32 devices in a mesh: dp: 4 (over z), ctx: 8 (over y, x, core).
Axes of the slice: x: 2, y: 2, z: 4, core: 2. Of those that a mesh axis runs over, the one named last changes fastest.
Arguments:
- output_gate_input: bfloat16 [4, 1024, 4096], P('dp', 'ctx'), may hold values from -6 to 6
- key_input: bfloat16 [4, 1024, 4096], P('dp', 'ctx'), may hold values from -6 to 6
- value_input: bfloat16 [4, 1024, 4096], P('dp', 'ctx'), may hold values from -6 to 6
- upstream: bfloat16 [4, 1024, 4096], P('dp', 'ctx'), may hold values from -6 to 6
- filter_taps: float32 [256, 1024], P('ctx'), may hold values from -6 to 6
- block_of_shard: int32 [8], replicated, may hold values from 0 to 7, each once
Outputs:
- mixed_out: bfloat16 [4, 1024, 4096], P('dp', 'ctx')
- gate_grad: bfloat16 [4, 1024, 4096], P('dp', 'ctx')
- key_grad: bfloat16 [4, 1024, 4096], P('dp', 'ctx')
- value_grad: bfloat16 [4, 1024, 4096], P('dp', 'ctx')
- taps_grad: float32 [256, 1024], P('ctx')
The draws below stay inside these ranges and needn't reach their ends.
Inputs may be any that keep to these rules, and one draw needn't show every extreme that they name: block_of_shard names every block of positions exactly once.
All inputs are finite; a program needn't handle non-finite values.
Results may differ from the reference program's by a relative error of at most 0.012.
Values may be sent and summed in bfloat16 or wider, within the bound.
A program may use at most 192 MiB of HBM per device.

```python
import math
import jax
import jax.numpy as jnp
from jax import lax

D = 4096
GROUP = 16
SEQ = 1024
SEQS = 4
POSITION_BLOCKS = 8
FILTERS = 256
N_DP = 4


def draw_filter_taps(key, part):
    subkeys = jax.random.split(key, 6)
    delay_positions = jnp.arange(SEQ, dtype=jnp.float32)[None, :]
    decay_length = jnp.exp(jax.random.uniform(subkeys[1], (FILTERS, 1), minval=math.log(30.0), maxval=math.log(4.0 * SEQ)))
    base_vals = jax.random.truncated_normal(subkeys[3], -6.0, 6.0, (FILTERS, SEQ))
    token_positions = jax.random.randint(subkeys[4], (FILTERS, 3, 1), 1, SEQ).astype(jnp.float32)
    envelope_factors = jax.random.uniform(subkeys[5], (FILTERS, 3, 1), minval=0.5, maxval=0.8)
    spike_step_count = jnp.where(delay_positions[:, None, :] >= token_positions, envelope_factors, 1.0)
    decay_envelope = jnp.exp(-delay_positions / decay_length) * jnp.prod(spike_step_count, axis=1)
    return (base_vals * decay_envelope).astype(jnp.float32)


def levels(key, shape, cuts, least, largest):
    def one(axis_at, blocks):
        steps = jax.random.uniform(jax.random.fold_in(jax.random.fold_in(key, 6), axis_at), (blocks,), jnp.float32, least / len(cuts), largest / len(cuts))
        return jnp.repeat(jnp.exp(steps), shape[axis_at] // blocks).reshape((-1,) + (1,) * (len(shape) - axis_at - 1))

    gain = one(*cuts[0])
    for cut in cuts[1:]:
        gain = gain * one(*cut)
    return gain


def noise(own_key, extent, width, limit, cuts=(), kind=jnp.bfloat16):
    gain = levels(own_key, extent, cuts, -0.22, 0.18) if cuts else 1.0
    result = jax.random.normal(own_key, extent, jnp.float32) * width * gain
    return jnp.minimum(jnp.maximum(result, -limit), limit).astype(kind)


def setup_inputs(seed: int = 0) -> dict:
    splits = jax.random.split(jax.random.key(seed), 7)
    output_gate_input = noise(splits[0], (SEQS, SEQ, D), 1.0, 6.0, ((0, 4), (1, 8)))
    key_input = noise(splits[1], (SEQS, SEQ, D), 1.0, 6.0, ((0, 4), (1, 8)))
    value_input = noise(splits[2], (SEQS, SEQ, D), 1.0, 6.0, ((0, 4), (1, 8)))
    upstream = noise(splits[3], (SEQS, SEQ, D), 1.0, 6.0, ((0, 4), (1, 8)))
    filter_taps = draw_filter_taps(jax.random.fold_in(splits[6], 71), 0)
    block_of_shard = jax.random.permutation(splits[5], POSITION_BLOCKS).astype(jnp.int32)
    return dict(output_gate_input=output_gate_input, key_input=key_input, value_input=value_input, upstream=upstream, filter_taps=filter_taps, block_of_shard=block_of_shard)


epsilon = 1e-06

def inverse_order(block_of_shard):
    pieces = block_of_shard.shape[0]
    labels = jnp.arange(pieces, dtype=jnp.int32)
    matches = (block_of_shard[:, None] == labels[None, :]).astype(jnp.int32)
    return lax.optimization_barrier(jnp.sum(labels[:, None] * matches, axis=0)).astype(jnp.int32)

def reorder_blocks(row_data, placing):
    pieces = placing.shape[0]
    shaped = row_data.reshape((pieces, row_data.shape[0] // pieces) + row_data.shape[1:])
    return jnp.take(shaped, placing, axis=0).reshape(row_data.shape)

def rounded(values):
    return lax.optimization_barrier(values.astype(jnp.bfloat16)).astype(jnp.float32)

def reference(output_gate_input, key_input, value_input, upstream, filter_taps, block_of_shard):
    length = filter_taps.shape[1]
    filters = filter_taps.shape[0]
    inverse = inverse_order(block_of_shard)
    taps = filter_taps.astype(jnp.float32)
    root_mean = jnp.sqrt(lax.optimization_barrier(jnp.mean(taps * taps, axis=1, keepdims=True)) + epsilon)
    norm_scale = 1.0 / (math.sqrt(length) * root_mean)
    kernel = rounded(taps * norm_scale)
    kernel_freq = jnp.fft.rfft(jnp.repeat(kernel.T, GROUP, axis=1), n=2 * length, axis=0)

    def per_sequence(inputs):
        gates, keys_in, values_in, grads_up = [reorder_blocks(member, inverse).astype(jnp.float32) for member in inputs]
        product = rounded(keys_in * values_in)
        product_freq = jnp.fft.rfft(product, n=2 * length, axis=0)
        mixing = rounded(jnp.fft.irfft(product_freq * kernel_freq, n=2 * length, axis=0)[:length])
        weighted = rounded(grads_up * gates)
        weighted_freq = jnp.fft.rfft(weighted, n=2 * length, axis=0)
        returned = rounded(jnp.fft.irfft(jnp.conj(kernel_freq) * weighted_freq, n=2 * length, axis=0)[:length])
        lag_sums = jnp.fft.irfft(weighted_freq * jnp.conj(product_freq), n=2 * length, axis=0)[:length]
        lag_sums = lax.optimization_barrier(jnp.sum(lag_sums.reshape(length, filters, GROUP), axis=2)).T
        results = (gates * mixing, grads_up * mixing, returned * values_in, returned * keys_in)
        results = tuple((reorder_blocks(member.astype(jnp.bfloat16), block_of_shard) for member in results))
        return results + (lag_sums,)
    mixed, gate_grad, key_grad, value_grad, lag_all = lax.map(per_sequence, (output_gate_input, key_input, value_input, upstream))
    lag_mean = lax.optimization_barrier(jnp.sum(lag_all, axis=0)) / N_DP
    projection = lax.optimization_barrier(jnp.sum(lag_mean * taps, axis=1, keepdims=True))
    taps_grad = norm_scale * lag_mean - taps * (norm_scale * norm_scale * norm_scale) * projection
    return (mixed, gate_grad, key_grad, value_grad, taps_grad)
```

```python
import functools
import math

import jax
import jax.numpy as jnp
from jax import lax
from jax.experimental import pallas as pl
from jax.experimental.pallas import tpu as pltpu
from jax.sharding import PartitionSpec as P

epsilon = 1e-06
F32 = jnp.float32
BF16 = jnp.bfloat16


def gate_product(first, second):
    return (first.astype(F32) * second.astype(F32)).astype(BF16)


def toeplitz_table(row, rows):
    length = row.shape[1]
    spread = jnp.broadcast_to(row, (rows, length))
    rolled = pltpu.roll(spread, 0, 1, stride=1, stride_axis=0)
    lag = lax.broadcasted_iota(jnp.int32, (rows, rows), 1) - lax.broadcasted_iota(
        jnp.int32, (rows, rows), 0
    )
    first = jnp.where(lag >= 0, rolled[:, :rows], 0.0)
    return jnp.concatenate([first, rolled[:, rows:]], axis=1).astype(BF16)


def diagonal_sums(square):
    rows, length = square.shape
    lag = lax.broadcasted_iota(jnp.int32, (rows, rows), 1) - lax.broadcasted_iota(
        jnp.int32, (rows, rows), 0
    )
    first = jnp.where(lag >= 0, square[:, :rows], 0.0)
    total = jnp.concatenate([first, square[:, rows:]], axis=1)
    half = rows // 2
    while half >= 8:
        total = total[:half] + pltpu.roll(total[half:], length - half, 1)
        half //= 2
    while half >= 1:
        total = total + pltpu.roll(pltpu.roll(total, length - half, 1), 8 - half, 0)
        half //= 2
    return total[:1]


def shifted(ref, which, lines, table, pieces):
    columns = []
    for lag in range(pieces):
        tiles = [ref[table[d, lag], which, lines, :] for d in range(pieces)]
        columns.append(jnp.concatenate(tiles, axis=0))
    return jnp.concatenate(columns, axis=1)


def group_work(ref, lines, back, ahead, table, pieces):
    rows = table.shape[0]
    signal = shifted(ref, 0, lines, back, pieces)
    weighted = shifted(ref, 1, lines, ahead, pieces)
    stacked = jnp.concatenate(
        [table[:, l * rows : (l + 1) * rows] for l in range(pieces)], axis=0
    )
    mixing = jnp.dot(signal, stacked, preferred_element_type=F32)
    returned = lax.dot_general(
        weighted, table, (((1,), (1,)), ((), ())), preferred_element_type=F32
    )
    square = lax.dot_general(
        signal[:, :rows], weighted, (((0,), (0,)), ((), ())), preferred_element_type=F32
    )
    return mixing.astype(BF16), returned.astype(BF16), diagonal_sums(square)


def core(back, ahead, taps_ref, xw_ref, out_ref, lag_ref):
    pieces = out_ref.shape[0]
    groups, length = taps_ref.shape
    rows = out_ref.shape[3]
    size = out_ref.shape[2] // groups

    @pl.loop(0, groups)
    def _(g):
        taps = taps_ref[pl.ds(g, 1), :]
        mean = jnp.mean(taps * taps, axis=1, keepdims=True)
        scale = 1.0 / (math.sqrt(length) * jnp.sqrt(mean + epsilon))
        kernel = (taps * scale).astype(BF16).astype(F32)
        table = toeplitz_table(kernel, rows)
        lines = pl.ds(pl.multiple_of(g * size, size), size)
        mixing, returned, lags = group_work(xw_ref, lines, back, ahead, table, pieces)
        for d in range(pieces):
            out_ref[d, 0, lines, :] = mixing[d * size : (d + 1) * size]
            out_ref[d, 1, lines, :] = returned[d * size : (d + 1) * size]
        lag_ref[pl.ds(g, 1), :] = lags


def block_tables(block_of_shard):
    pieces = block_of_shard.shape[0]
    labels = jnp.arange(pieces, dtype=jnp.int32)
    lags = labels[None, :]

    def slot(block):
        matches = (block[:, :, None] == block_of_shard[None, None, :]).astype(jnp.int32)
        found = jnp.sum(matches * labels, axis=2)
        return jnp.where(jnp.sum(matches, axis=2) > 0, found, pieces)

    here = block_of_shard[:, None]
    return slot(here - lags), slot(here + lags)


def shards(output_gate_input, key_input, value_input, upstream, filter_taps, block_of_shard):
    groups, length = filter_taps.shape
    pieces = block_of_shard.shape[0]
    gates, keys, values, grads = (
        member[0] for member in (output_gate_input, key_input, value_input, upstream)
    )
    rows, width = gates.shape
    channels = width // pieces
    back, ahead = block_tables(block_of_shard)
    pair = jnp.stack(
        [
            gate_product(keys, values).T.reshape(pieces, channels, rows),
            gate_product(grads, gates).T.reshape(pieces, channels, rows),
        ],
        axis=1,
    )
    arrived = lax.all_to_all(pair, "ctx", split_axis=0, concat_axis=0, tiled=True)
    arrived = jnp.pad(arrived, ((0, 1), (0, 0), (0, 0), (0, 0)))
    vmem = pl.BlockSpec(memory_space=pltpu.VMEM)
    smem = pl.BlockSpec(memory_space=pltpu.SMEM)
    results, lag_sums = pl.pallas_call(
        core,
        out_shape=(
            jax.ShapeDtypeStruct((pieces, 2, channels, rows), BF16),
            jax.ShapeDtypeStruct((groups, length), F32),
        ),
        in_specs=[smem, smem, vmem, vmem],
        out_specs=(vmem, vmem),
        compiler_params=pltpu.CompilerParams(vmem_limit_bytes=56 * 1024 * 1024),
    )(back, ahead, filter_taps, arrived)
    home = lax.all_to_all(results, "ctx", split_axis=0, concat_axis=0, tiled=True)
    mixing = home[:, 0].reshape(width, rows).T
    returned = home[:, 1].reshape(width, rows).T
    lag_mean = lax.psum(lag_sums, "dp") / lax.axis_size("dp")
    root_mean = jnp.sqrt(jnp.mean(filter_taps * filter_taps, axis=1, keepdims=True) + epsilon)
    norm_scale = 1.0 / (math.sqrt(length) * root_mean)
    projection = jnp.sum(lag_mean * filter_taps, axis=1, keepdims=True)
    taps_grad = (
        norm_scale * lag_mean - filter_taps * (norm_scale * norm_scale * norm_scale) * projection
    )
    return (
        gate_product(gates, mixing)[None],
        gate_product(grads, mixing)[None],
        gate_product(returned, values)[None],
        gate_product(returned, keys)[None],
        taps_grad,
    )


def solution(mesh):
    wide = P("dp", "ctx", None)
    return jax.shard_map(
        shards,
        mesh=mesh,
        in_specs=(wide, wide, wide, wide, P("ctx", None), P()),
        out_specs=(wide, wide, wide, wide, P("ctx", None)),
        check_vma=False,
    )
```

```python
import functools
import math

import jax
import jax.numpy as jnp
from jax import lax
from jax.experimental import pallas as pl
from jax.experimental.pallas import tpu as pltpu
from jax.sharding import PartitionSpec as P

epsilon = 1e-06
F32 = jnp.float32
BF16 = jnp.bfloat16
EARLY = 2


def gate_product(first, second):
    return (first.astype(F32) * second.astype(F32)).astype(BF16)


def toeplitz_table(row, rows):
    length = row.shape[1]
    spread = jnp.broadcast_to(row, (rows, length))
    rolled = pltpu.roll(spread, 0, 1, stride=1, stride_axis=0)
    lag = lax.broadcasted_iota(jnp.int32, (rows, rows), 1) - lax.broadcasted_iota(
        jnp.int32, (rows, rows), 0
    )
    first = jnp.where(lag >= 0, rolled[:, :rows], 0.0)
    return jnp.concatenate([first, rolled[:, rows:]], axis=1).astype(BF16)


def diagonal_sums(square):
    rows, length = square.shape
    lag = lax.broadcasted_iota(jnp.int32, (rows, rows), 1) - lax.broadcasted_iota(
        jnp.int32, (rows, rows), 0
    )
    first = jnp.where(lag >= 0, square[:, :rows], 0.0)
    total = jnp.concatenate([first, square[:, rows:]], axis=1)
    half = rows // 2
    while half >= 8:
        total = total[:half] + pltpu.roll(total[half:], length - half, 1)
        half //= 2
    while half >= 1:
        total = total + pltpu.roll(pltpu.roll(total, length - half, 1), 8 - half, 0)
        half //= 2
    return total[:1]


def shifted(ref, which, lines, places_ref, step, pieces):
    columns = []
    for lag in range(pieces):
        tiles = []
        for d in range(pieces):
            place = places_ref[places_ref[4 * pieces + d] + (pieces + step * lag)]
            tiles.append(ref[place, which, lines, :])
        columns.append(jnp.concatenate(tiles, axis=0))
    return jnp.concatenate(columns, axis=1)


def group_work(ref, lines, places_ref, table, pieces):
    rows = table.shape[0]
    signal = shifted(ref, 0, lines, places_ref, -1, pieces)
    weighted = shifted(ref, 1, lines, places_ref, 1, pieces)
    stacked = jnp.concatenate(
        [table[:, l * rows : (l + 1) * rows] for l in range(pieces)], axis=0
    )
    mixing = jnp.dot(signal, stacked, preferred_element_type=F32)
    returned = lax.dot_general(
        weighted, table, (((1,), (1,)), ((), ())), preferred_element_type=F32
    )
    square = lax.dot_general(
        signal[:, :rows], weighted, (((0,), (0,)), ((), ())), preferred_element_type=F32
    )
    return mixing.astype(BF16), returned.astype(BF16), diagonal_sums(square)


def scale_of(taps):
    mean = jnp.mean(taps * taps, axis=1, keepdims=True)
    return 1.0 / (math.sqrt(taps.shape[1]) * jnp.sqrt(mean + epsilon))


def layer(
    waves, pieces, copies,
    block_ref, taps_ref, gates_ref, keys_ref, values_ref, grads_ref,
    mixing_ref, returned_ref, taps_grad_ref,
    places_ref, tables_ref, *rest,
):
    sends, recvs, results, homes, lags = (rest[i * waves : (i + 1) * waves] for i in range(5))
    out_sem, in_sem, back_sem, home_sem, lag_out_sem, lag_in_sem = rest[5 * waves :]
    me = lax.axis_index("ctx")
    me_dp = lax.axis_index("dp")
    rows, width = gates_ref.shape
    channels = width // pieces
    part = channels // waves
    groups = taps_ref.shape[0]
    size = channels // groups
    each = groups // waves

    barrier = pltpu.get_barrier_semaphore()

    @pl.loop(1, pieces)
    def _(o):
        pl.semaphore_signal(
            barrier, inc=1, device_id={"ctx": lax.rem(me + o, pieces)}, device_id_type=pl.DeviceIdType.MESH
        )

    @pl.loop(1, copies)
    def _(o):
        pl.semaphore_signal(
            barrier, inc=1, device_id={"dp": lax.rem(me_dp + o, copies)}, device_id_type=pl.DeviceIdType.MESH
        )

    def prepare(w, d, ref, slot):
        columns = pl.ds(pl.multiple_of(d * channels + w * part, 128), part)
        ref[slot, 0] = gate_product(keys_ref[:, columns], values_ref[:, columns]).T
        ref[slot, 1] = gate_product(grads_ref[:, columns], gates_ref[:, columns]).T

    def outward(w, d):
        return pltpu.make_async_remote_copy(
            src_ref=sends[w].at[d], dst_ref=recvs[w].at[me],
            send_sem=out_sem.at[w, d], recv_sem=in_sem.at[w, me],
            device_id={"ctx": d}, device_id_type=pl.DeviceIdType.MESH,
        )

    def inward(w, d):
        return pltpu.make_async_remote_copy(
            src_ref=sends[w].at[d], dst_ref=recvs[w].at[d],
            send_sem=out_sem.at[w, d], recv_sem=in_sem.at[w, d],
            device_id={"ctx": d}, device_id_type=pl.DeviceIdType.MESH,
        )

    def homeward(w, d):
        return pltpu.make_async_remote_copy(
            src_ref=results[w].at[d], dst_ref=homes[w].at[me],
            send_sem=back_sem.at[w, d], recv_sem=home_sem.at[w, me],
            device_id={"ctx": d}, device_id_type=pl.DeviceIdType.MESH,
        )

    def arriving(w, d):
        return pltpu.make_async_remote_copy(
            src_ref=results[w].at[d], dst_ref=homes[w].at[d],
            send_sem=back_sem.at[w, d], recv_sem=home_sem.at[w, d],
            device_id={"ctx": d}, device_id_type=pl.DeviceIdType.MESH,
        )

    def lag_copy(w, d, slot):
        return pltpu.make_async_remote_copy(
            src_ref=lags[w].at[me_dp], dst_ref=lags[w].at[slot],
            send_sem=lag_out_sem.at[w, d], recv_sem=lag_in_sem.at[w, slot],
            device_id={"dp": d}, device_id_type=pl.DeviceIdType.MESH,
        )

    @pl.loop(1, pieces)
    def _(o):
        d = lax.rem(me + o, pieces)
        prepare(0, d, sends[0], d)

    pl.semaphore_wait(barrier, pieces + copies - 2)

    @pl.loop(1, pieces)
    def _(o):
        outward(0, lax.rem(me + o, pieces)).start()

    for w in range(1, waves):

        @pl.loop(1, pieces)
        def _(o):
            d = lax.rem(me + o, pieces)
            prepare(w, d, sends[w], d)
            outward(w, d).start()

    for w in range(waves):
        prepare(w, me, recvs[w], me)
        recvs[w][pieces] = jnp.zeros((2, part, rows), BF16)

    @pl.loop(0, 4 * pieces)
    def _(i):
        places_ref[i] = pieces

    @pl.loop(0, pieces)
    def _(b):
        found = 0
        for d in range(pieces):
            found = jnp.where(block_ref[d] == b, d, found)
        places_ref[pieces + b] = found
        places_ref[4 * pieces + b] = block_ref[b]

    def build(g):
        taps = taps_ref[pl.ds(g, 1), :]
        kernel = (taps * scale_of(taps)).astype(BF16).astype(F32)
        return toeplitz_table(kernel, rows)

    early = min(EARLY, waves)

    @pl.loop(0, early * each)
    def _(g):
        tables_ref[g] = build(g)

    def unload(w):
        @pl.loop(1, pieces)
        def _(o):
            arriving(w, lax.rem(me + pieces - o, pieces)).wait_recv()

        @pl.loop(0, pieces)
        def _(d):
            columns = pl.ds(pl.multiple_of(d * channels + w * part, 128), part)
            mixing_ref[:, columns] = homes[w][d, 0].T
            returned_ref[:, columns] = homes[w][d, 1].T

    for w in range(waves):

        @pl.loop(1, pieces)
        def _(o):
            inward(w, lax.rem(me + pieces - o, pieces)).wait_recv()

        @pl.loop(0, each)
        def _(i):
            g = w * each + i
            table = tables_ref[g] if w < early else build(g)
            lines = pl.ds(pl.multiple_of(i * size, size), size)
            mixing, returned, sums = group_work(recvs[w], lines, places_ref, table, pieces)
            for d in range(pieces):
                results[w][d, 0, lines, :] = mixing[d * size : (d + 1) * size]
                results[w][d, 1, lines, :] = returned[d * size : (d + 1) * size]
            lags[w][me_dp, pl.ds(i, 1), :] = sums

        @pl.loop(1, pieces)
        def _(o):
            homeward(w, lax.rem(me + o, pieces)).start()

        @pl.loop(1, copies)
        def _(o):
            lag_copy(w, lax.rem(me_dp + o, copies), me_dp).start()

        homes[w][me] = results[w][me]
        if w > 0:
            unload(w - 1)

    def finish(w):
        @pl.loop(1, copies)
        def _(o):
            d = lax.rem(me_dp + copies - o, copies)
            lag_copy(w, d, d).wait_recv()

        total = lags[w][0]
        for i in range(1, copies):
            total = total + lags[w][i]
        mean = total / copies
        taps = taps_ref[w * each : (w + 1) * each, :]
        scale = scale_of(taps)
        projection = jnp.sum(mean * taps, axis=1, keepdims=True)
        taps_grad_ref[w * each : (w + 1) * each, :] = (
            scale * mean - taps * (scale * scale * scale) * projection
        )

    for w in range(waves - 1):
        finish(w)
    unload(waves - 1)
    finish(waves - 1)

    for w in range(waves):

        @pl.loop(1, pieces)
        def _(o):
            d = lax.rem(me + o, pieces)
            outward(w, d).wait_send()
            homeward(w, d).wait_send()

        @pl.loop(1, copies)
        def _(o):
            lag_copy(w, lax.rem(me_dp + o, copies), me_dp).wait_send()


def shards(output_gate_input, key_input, value_input, upstream, filter_taps, block_of_shard):
    groups, length = filter_taps.shape
    pieces = block_of_shard.shape[0]
    copies = lax.axis_size("dp")
    gates, keys, values, grads = (
        member[0] for member in (output_gate_input, key_input, value_input, upstream)
    )
    rows, width = gates.shape
    channels = width // pieces
    part = 128
    waves = channels // part
    each = groups // waves
    vmem = pl.BlockSpec(memory_space=pltpu.VMEM)
    smem = pl.BlockSpec(memory_space=pltpu.SMEM)
    slots = pltpu.VMEM((pieces, 2, part, rows), BF16)
    ctx_sems = pltpu.SemaphoreType.DMA((waves, pieces))
    dp_sems = pltpu.SemaphoreType.DMA((waves, copies))
    mixing, returned, taps_grad = pl.pallas_call(
        functools.partial(layer, waves, pieces, copies),
        out_shape=(
            jax.ShapeDtypeStruct((rows, width), BF16),
            jax.ShapeDtypeStruct((rows, width), BF16),
            jax.ShapeDtypeStruct((groups, length), F32),
        ),
        in_specs=[smem] + [vmem] * 5,
        out_specs=(vmem,) * 3,
        scratch_shapes=[
            pltpu.SMEM((5 * pieces,), jnp.int32),
            pltpu.VMEM((min(EARLY, waves) * each, rows, length), BF16),
            *([slots] * waves),
            *([pltpu.VMEM((pieces + 1, 2, part, rows), BF16)] * waves),
            *([slots] * waves),
            *([slots] * waves),
            *([pltpu.VMEM((copies, each, length), F32)] * waves),
            ctx_sems, ctx_sems, ctx_sems, ctx_sems, dp_sems, dp_sems,
        ],
        compiler_params=pltpu.CompilerParams(
            vmem_limit_bytes=56 * 1024 * 1024, collective_id=0, has_side_effects=True
        ),
        cost_estimate=pl.CostEstimate(
            flops=6 * channels * length * length, bytes_accessed=12 * rows * width, transcendentals=0
        ),
    )(block_of_shard, filter_taps, gates, keys, values, grads)
    return (
        gate_product(gates, mixing)[None],
        gate_product(grads, mixing)[None],
        gate_product(returned, values)[None],
        gate_product(returned, keys)[None],
        taps_grad,
    )


def solution(mesh):
    wide = P("dp", "ctx", None)
    return jax.shard_map(
        shards,
        mesh=mesh,
        in_specs=(wide, wide, wide, wide, P("ctx", None), P()),
        out_specs=(wide, wide, wide, wide, P("ctx", None)),
        check_vma=False,
    )
```

```python
import functools
import math

import jax
import jax.numpy as jnp
from jax import lax
from jax.experimental import pallas as pl
from jax.experimental.pallas import tpu as pltpu
from jax.sharding import PartitionSpec as P

epsilon = 1e-06
F32 = jnp.float32
BF16 = jnp.bfloat16
EARLY = 2


def gate_product(first, second):
    return (first.astype(F32) * second.astype(F32)).astype(BF16)


def toeplitz_table(row, rows):
    length = row.shape[1]
    spread = jnp.broadcast_to(row, (rows, length))
    rolled = pltpu.roll(spread, 0, 1, stride=1, stride_axis=0)
    lag = lax.broadcasted_iota(jnp.int32, (rows, rows), 1) - lax.broadcasted_iota(
        jnp.int32, (rows, rows), 0
    )
    first = jnp.where(lag >= 0, rolled[:, :rows], 0.0)
    return jnp.concatenate([first, rolled[:, rows:]], axis=1).astype(BF16)


def diagonal_sums(square):
    rows, length = square.shape
    total_index = lax.broadcasted_iota(jnp.int32, (rows, rows), 0) + lax.broadcasted_iota(
        jnp.int32, (rows, rows), 1
    )
    last = jnp.where(total_index < rows, square[:, length - rows :], 0.0)
    total = jnp.concatenate([square[:, : length - rows], last], axis=1)
    half = rows // 2
    while half >= 8:
        total = total[:half] + pltpu.roll(total[half:], half, 1)
        half //= 2
    while half >= 1:
        total = total + pltpu.roll(pltpu.roll(total, half, 1), 8 - half, 0)
        half //= 2
    return total[:1]


def turning(rows, kind):
    total_index = lax.broadcasted_iota(jnp.int32, (rows, rows), 0) + lax.broadcasted_iota(
        jnp.int32, (rows, rows), 1
    )
    return jnp.where(total_index == rows - 1, 1.0, 0.0).astype(kind)


def group_work(signal, weighted, table, pieces):
    lines, rows = signal.shape
    size = lines // pieces

    def later(l):
        return jnp.concatenate([jnp.zeros((l * size, rows), BF16), signal[: lines - l * size]], axis=0) if l else signal

    def earlier(l):
        return jnp.concatenate([weighted[l * size :], jnp.zeros((l * size, rows), BF16)], axis=0) if l else weighted

    ahead = [earlier(l) for l in range(pieces)]
    both = jnp.concatenate(
        [jnp.concatenate([later(l), ahead[l]], axis=0) for l in range(pieces)], axis=1
    )
    stacked = jnp.concatenate(
        [table[:, l * rows : (l + 1) * rows] for l in range(pieces)], axis=0
    )
    filtered = jnp.dot(both, stacked, preferred_element_type=F32).astype(BF16)
    square = lax.dot_general(
        signal,
        jnp.concatenate(ahead[::-1], axis=1),
        (((0,), (0,)), ((), ())),
        preferred_element_type=F32,
    )
    return filtered[:lines], filtered[lines:], diagonal_sums(square)


def scale_of(taps):
    mean = jnp.mean(taps * taps, axis=1, keepdims=True)
    return 1.0 / (math.sqrt(taps.shape[1]) * jnp.sqrt(mean + epsilon))


def layer(
    waves, pieces, copies,
    block_ref, taps_ref, gates_ref, keys_ref, values_ref, grads_ref,
    mixing_ref, returned_ref, taps_grad_ref,
    places_ref, tables_ref, ordered_ref, filtered_ref, *rest,
):
    sends, recvs, results, homes, lags = (rest[i * waves : (i + 1) * waves] for i in range(5))
    out_sem, in_sem, back_sem, home_sem, lag_out_sem, lag_in_sem = rest[5 * waves :]
    me = lax.axis_index("ctx")
    me_dp = lax.axis_index("dp")
    rows, width = gates_ref.shape
    channels = width // pieces
    part = channels // waves
    groups = taps_ref.shape[0]
    size = channels // groups
    each = groups // waves
    turn = turning(rows, BF16)
    pair = 2 if pieces <= 8 and each % 2 == 0 else 1

    barrier = pltpu.get_barrier_semaphore()

    @pl.loop(1, pieces)
    def _(o):
        pl.semaphore_signal(
            barrier, inc=1, device_id={"ctx": lax.rem(me + o, pieces)}, device_id_type=pl.DeviceIdType.MESH
        )

    @pl.loop(1, copies)
    def _(o):
        pl.semaphore_signal(
            barrier, inc=1, device_id={"dp": lax.rem(me_dp + o, copies)}, device_id_type=pl.DeviceIdType.MESH
        )

    def prepare(w, d, ref, slot):
        columns = pl.ds(pl.multiple_of(d * channels + w * part, 128), part)
        ref[slot, 0] = gate_product(keys_ref[:, columns], values_ref[:, columns]).T
        ref[slot, 1] = lax.dot_general(
            gate_product(grads_ref[:, columns], gates_ref[:, columns]), turn,
            (((0,), (0,)), ((), ())), preferred_element_type=F32,
        ).astype(BF16)

    def outward(w, d):
        return pltpu.make_async_remote_copy(
            src_ref=sends[w].at[d], dst_ref=recvs[w].at[me],
            send_sem=out_sem.at[w, d], recv_sem=in_sem.at[w, me],
            device_id={"ctx": d}, device_id_type=pl.DeviceIdType.MESH,
        )

    def inward(w, d):
        return pltpu.make_async_remote_copy(
            src_ref=sends[w].at[d], dst_ref=recvs[w].at[d],
            send_sem=out_sem.at[w, d], recv_sem=in_sem.at[w, d],
            device_id={"ctx": d}, device_id_type=pl.DeviceIdType.MESH,
        )

    def homeward(w, d):
        return pltpu.make_async_remote_copy(
            src_ref=results[w].at[d], dst_ref=homes[w].at[me],
            send_sem=back_sem.at[w, d], recv_sem=home_sem.at[w, me],
            device_id={"ctx": d}, device_id_type=pl.DeviceIdType.MESH,
        )

    def arriving(w, d):
        return pltpu.make_async_remote_copy(
            src_ref=results[w].at[d], dst_ref=homes[w].at[d],
            send_sem=back_sem.at[w, d], recv_sem=home_sem.at[w, d],
            device_id={"ctx": d}, device_id_type=pl.DeviceIdType.MESH,
        )

    def lag_copy(w, d, slot):
        return pltpu.make_async_remote_copy(
            src_ref=lags[w].at[me_dp], dst_ref=lags[w].at[slot],
            send_sem=lag_out_sem.at[w, d], recv_sem=lag_in_sem.at[w, slot],
            device_id={"dp": d}, device_id_type=pl.DeviceIdType.MESH,
        )

    @pl.loop(1, pieces)
    def _(o):
        d = lax.rem(me + o, pieces)
        prepare(0, d, sends[0], d)

    pl.semaphore_wait(barrier, pieces + copies - 2)

    @pl.loop(1, pieces)
    def _(o):
        outward(0, lax.rem(me + o, pieces)).start()

    for w in range(1, waves):

        @pl.loop(1, pieces)
        def _(o):
            d = lax.rem(me + o, pieces)
            prepare(w, d, sends[w], d)
            outward(w, d).start()

    for w in range(waves):
        prepare(w, me, recvs[w], me)

    @pl.loop(0, pieces)
    def _(b):
        found = 0
        for d in range(pieces):
            found = jnp.where(block_ref[d] == b, d, found)
        places_ref[b] = found

    def build(g):
        taps = taps_ref[pl.ds(g, 1), :]
        kernel = (taps * scale_of(taps)).astype(BF16).astype(F32)
        return toeplitz_table(kernel, rows)

    early = min(EARLY, waves)

    @pl.loop(0, early * each // pair)
    def _(i):
        made = [build(i * pair + k) for k in range(pair)]
        for k in range(pair):
            tables_ref[i * pair + k] = made[k]

    def unload(w):
        @pl.loop(1, pieces)
        def _(o):
            arriving(w, lax.rem(me + pieces - o, pieces)).wait_recv()

        @pl.loop(0, pieces)
        def _(d):
            columns = pl.ds(pl.multiple_of(d * channels + w * part, 128), part)
            mixing_ref[:, columns] = homes[w][d, 0].T
            returned_ref[:, columns] = lax.dot_general(
                turn, homes[w][d, 1], (((1,), (1,)), ((), ())), preferred_element_type=F32
            ).astype(BF16)

    for w in range(waves):

        @pl.loop(1, pieces)
        def _(o):
            inward(w, lax.rem(me + pieces - o, pieces)).wait_recv()

        @pl.loop(0, pieces)
        def _(b):
            ordered_ref[b] = recvs[w][places_ref[b]]

        @pl.loop(0, each // pair)
        def _(i):
            made = []
            for k in range(pair):
                g = i * pair + k
                table = tables_ref[w * each + g] if w < early else build(w * each + g)
                lines = pl.ds(pl.multiple_of(g * size, size), size)
                signal = ordered_ref[:, 0, lines, :].reshape(pieces * size, rows)
                weighted = ordered_ref[:, 1, lines, :].reshape(pieces * size, rows)
                made.append((g, lines, *group_work(signal, weighted, table, pieces)))
            for g, lines, mixing, returned, sums in made:
                filtered_ref[:, 0, lines, :] = mixing.reshape(pieces, size, rows)
                filtered_ref[:, 1, lines, :] = returned.reshape(pieces, size, rows)
                lags[w][me_dp, pl.ds(g, 1), :] = sums

        @pl.loop(0, pieces)
        def _(d):
            results[w][d] = filtered_ref[block_ref[d]]

        @pl.loop(1, pieces)
        def _(o):
            homeward(w, lax.rem(me + o, pieces)).start()

        @pl.loop(1, copies)
        def _(o):
            lag_copy(w, lax.rem(me_dp + o, copies), me_dp).start()

        homes[w][me] = results[w][me]
        if w > 0:
            unload(w - 1)

    def finish(w):
        @pl.loop(1, copies)
        def _(o):
            d = lax.rem(me_dp + copies - o, copies)
            lag_copy(w, d, d).wait_recv()

        total = lags[w][0]
        for i in range(1, copies):
            total = total + lags[w][i]
        turned = turning(rows, F32)
        mean = jnp.concatenate(
            [
                jnp.dot(
                    total[:, l * rows : (l + 1) * rows], turned,
                    precision=lax.Precision.HIGHEST, preferred_element_type=F32,
                )
                for l in reversed(range(pieces))
            ],
            axis=1,
        ) / copies
        taps = taps_ref[w * each : (w + 1) * each, :]
        scale = scale_of(taps)
        projection = jnp.sum(mean * taps, axis=1, keepdims=True)
        taps_grad_ref[w * each : (w + 1) * each, :] = (
            scale * mean - taps * (scale * scale * scale) * projection
        )

    for w in range(waves - 1):
        finish(w)
    unload(waves - 1)
    finish(waves - 1)

    for w in range(waves):

        @pl.loop(1, pieces)
        def _(o):
            d = lax.rem(me + o, pieces)
            outward(w, d).wait_send()
            homeward(w, d).wait_send()

        @pl.loop(1, copies)
        def _(o):
            lag_copy(w, lax.rem(me_dp + o, copies), me_dp).wait_send()


def shards(output_gate_input, key_input, value_input, upstream, filter_taps, block_of_shard):
    groups, length = filter_taps.shape
    pieces = block_of_shard.shape[0]
    copies = lax.axis_size("dp")
    gates, keys, values, grads = (
        member[0] for member in (output_gate_input, key_input, value_input, upstream)
    )
    rows, width = gates.shape
    channels = width // pieces
    part = 128
    waves = channels // part
    each = groups // waves
    vmem = pl.BlockSpec(memory_space=pltpu.VMEM)
    smem = pl.BlockSpec(memory_space=pltpu.SMEM)
    slots = pltpu.VMEM((pieces, 2, part, rows), BF16)
    ctx_sems = pltpu.SemaphoreType.DMA((waves, pieces))
    dp_sems = pltpu.SemaphoreType.DMA((waves, copies))
    mixing, returned, taps_grad = pl.pallas_call(
        functools.partial(layer, waves, pieces, copies),
        out_shape=(
            jax.ShapeDtypeStruct((rows, width), BF16),
            jax.ShapeDtypeStruct((rows, width), BF16),
            jax.ShapeDtypeStruct((groups, length), F32),
        ),
        in_specs=[smem] + [vmem] * 5,
        out_specs=(vmem,) * 3,
        scratch_shapes=[
            pltpu.SMEM((pieces,), jnp.int32),
            pltpu.VMEM((min(EARLY, waves) * each, rows, length), BF16),
            slots,
            slots,
            *([slots] * (4 * waves)),
            *([pltpu.VMEM((copies, each, length), F32)] * waves),
            ctx_sems, ctx_sems, ctx_sems, ctx_sems, dp_sems, dp_sems,
        ],
        compiler_params=pltpu.CompilerParams(
            vmem_limit_bytes=56 * 1024 * 1024, collective_id=0, has_side_effects=True
        ),
        cost_estimate=pl.CostEstimate(
            flops=6 * channels * length * length, bytes_accessed=12 * rows * width, transcendentals=0
        ),
    )(block_of_shard, filter_taps, gates, keys, values, grads)
    return (
        gate_product(gates, mixing)[None],
        gate_product(grads, mixing)[None],
        gate_product(returned, values)[None],
        gate_product(returned, keys)[None],
        taps_grad,
    )


def solution(mesh):
    wide = P("dp", "ctx", None)
    return jax.shard_map(
        shards,
        mesh=mesh,
        in_specs=(wide, wide, wide, wide, P("ctx", None), P()),
        out_specs=(wide, wide, wide, wide, P("ctx", None)),
        check_vma=False,
    )
```

```python
import functools
import math

import jax
import jax.numpy as jnp
from jax import lax
from jax.experimental import pallas as pl
from jax.experimental.pallas import tpu as pltpu
from jax.sharding import PartitionSpec as P

epsilon = 1e-06
F32 = jnp.float32
BF16 = jnp.bfloat16
EARLY = 2


def gate_product(first, second):
    return first * second


def toeplitz_table(row, rows):
    length = row.shape[1]
    spread = jnp.broadcast_to(row, (rows, length))
    rolled = pltpu.roll(spread, 0, 1, stride=1, stride_axis=0)
    lag = lax.broadcasted_iota(jnp.int32, (rows, rows), 1) - lax.broadcasted_iota(
        jnp.int32, (rows, rows), 0
    )
    first = jnp.where(lag >= 0, rolled[:, :rows], 0.0)
    return jnp.concatenate([first, rolled[:, rows:]], axis=1).astype(BF16)


def diagonal_sums(square):
    rows, length = square.shape
    total_index = lax.broadcasted_iota(jnp.int32, (rows, rows), 0) + lax.broadcasted_iota(
        jnp.int32, (rows, rows), 1
    )
    last = jnp.where(total_index < rows, square[:, length - rows :], 0.0)
    total = jnp.concatenate([square[:, : length - rows], last], axis=1)
    half = rows // 2
    while half >= 8:
        total = total[:half] + pltpu.roll(total[half:], half, 1)
        half //= 2
    while half >= 1:
        total = total + pltpu.roll(pltpu.roll(total, half, 1), 8 - half, 0)
        half //= 2
    return total[:1]


def turning(rows, kind):
    total_index = lax.broadcasted_iota(jnp.int32, (rows, rows), 0) + lax.broadcasted_iota(
        jnp.int32, (rows, rows), 1
    )
    return jnp.where(total_index == rows - 1, 1.0, 0.0).astype(kind)


def group_work(signal, weighted, table, pieces):
    lines, rows = signal.shape
    size = lines // pieces

    def later(l):
        return jnp.concatenate([jnp.zeros((l * size, rows), BF16), signal[: lines - l * size]], axis=0) if l else signal

    def earlier(l):
        return jnp.concatenate([weighted[l * size :], jnp.zeros((l * size, rows), BF16)], axis=0) if l else weighted

    ahead = [earlier(l) for l in range(pieces)]
    both = jnp.concatenate(
        [jnp.concatenate([later(l), ahead[l]], axis=0) for l in range(pieces)], axis=1
    )
    stacked = jnp.concatenate(
        [table[:, l * rows : (l + 1) * rows] for l in range(pieces)], axis=0
    )
    filtered = jnp.dot(both, stacked, preferred_element_type=F32).astype(BF16)
    square = lax.dot_general(
        signal,
        jnp.concatenate(ahead[::-1], axis=1),
        (((0,), (0,)), ((), ())),
        preferred_element_type=F32,
    )
    return filtered[:lines], filtered[lines:], diagonal_sums(square)


def scale_of(taps):
    mean = jnp.mean(taps * taps, axis=1, keepdims=True)
    return 1.0 / (math.sqrt(taps.shape[1]) * jnp.sqrt(mean + epsilon))


def exclusive_or(first, second, size):
    total, bit = 0, 1
    while bit < size:
        total = total + bit * lax.rem(first // bit + second // bit, 2)
        bit *= 2
    return total


def send_orders(pieces):
    half = pieces // 2
    chips = list(range(1, half))
    turned = [chips[1], chips[0], *chips[2:]] if len(chips) > 1 else chips
    one = [2 * c for c in chips] + [2 * c + 1 for c in chips] + [1]
    other = [2 * c + 1 for c in turned] + [2 * c for c in turned] + [1]
    return list(zip(one, other))


def partners(me, pieces):
    core = lax.rem(me, 2)
    for one, other in send_orders(pieces):
        yield exclusive_or(me, one + core * (other - one), pieces)


def products(gates, grads, keys, values, mixing, returned, taps, out, gate, key, value, taps_out):
    out[...] = gates[...] * mixing[...]
    gate[...] = grads[...] * mixing[...]
    key[...] = returned[...] * values[...]
    value[...] = returned[...] * keys[...]
    taps_out[...] = taps[...]


def layer(
    waves, pieces, copies,
    block_ref, taps_ref, gates_ref, keys_ref, values_ref, grads_ref,
    mixing_ref, returned_ref, taps_grad_ref,
    places_ref, tables_ref, ordered_ref, filtered_ref, *rest,
):
    sends, recvs, results, homes, lags = (rest[i * waves : (i + 1) * waves] for i in range(5))
    out_sem, in_sem, back_sem, home_sem, lag_out_sem, lag_in_sem = rest[5 * waves :]
    me = lax.axis_index("ctx")
    me_dp = lax.axis_index("dp")
    rows, width = gates_ref.shape
    channels = width // pieces
    part = channels // waves
    groups = taps_ref.shape[0]
    size = channels // groups
    each = groups // waves
    turn = turning(rows, BF16)
    pair = 2 if pieces <= 8 and each % 2 == 0 else 1

    barrier = pltpu.get_barrier_semaphore()

    @pl.loop(1, pieces)
    def _(o):
        pl.semaphore_signal(
            barrier, inc=1, device_id={"ctx": lax.rem(me + o, pieces)}, device_id_type=pl.DeviceIdType.MESH
        )

    @pl.loop(1, copies)
    def _(o):
        pl.semaphore_signal(
            barrier, inc=1, device_id={"dp": lax.rem(me_dp + o, copies)}, device_id_type=pl.DeviceIdType.MESH
        )

    def prepare(w, d, ref, slot):
        columns = pl.ds(pl.multiple_of(d * channels + w * part, 128), part)
        ref[slot, 0] = gate_product(keys_ref[:, columns], values_ref[:, columns]).T
        ref[slot, 1] = lax.dot_general(
            gate_product(grads_ref[:, columns], gates_ref[:, columns]), turn,
            (((0,), (0,)), ((), ())), preferred_element_type=F32,
        ).astype(BF16)

    def outward(w, d):
        return pltpu.make_async_remote_copy(
            src_ref=sends[w].at[d], dst_ref=recvs[w].at[me],
            send_sem=out_sem.at[w, d], recv_sem=in_sem.at[w, me],
            device_id={"ctx": d}, device_id_type=pl.DeviceIdType.MESH,
        )

    def inward(w, d):
        return pltpu.make_async_remote_copy(
            src_ref=sends[w].at[d], dst_ref=recvs[w].at[d],
            send_sem=out_sem.at[w, d], recv_sem=in_sem.at[w, d],
            device_id={"ctx": d}, device_id_type=pl.DeviceIdType.MESH,
        )

    def homeward(w, d):
        return pltpu.make_async_remote_copy(
            src_ref=results[w].at[d], dst_ref=homes[w].at[me],
            send_sem=back_sem.at[w, d], recv_sem=home_sem.at[w, me],
            device_id={"ctx": d}, device_id_type=pl.DeviceIdType.MESH,
        )

    def arriving(w, d):
        return pltpu.make_async_remote_copy(
            src_ref=results[w].at[d], dst_ref=homes[w].at[d],
            send_sem=back_sem.at[w, d], recv_sem=home_sem.at[w, d],
            device_id={"ctx": d}, device_id_type=pl.DeviceIdType.MESH,
        )

    def lag_copy(w, d, slot):
        return pltpu.make_async_remote_copy(
            src_ref=lags[w].at[me_dp], dst_ref=lags[w].at[slot],
            send_sem=lag_out_sem.at[w, d], recv_sem=lag_in_sem.at[w, slot],
            device_id={"dp": d}, device_id_type=pl.DeviceIdType.MESH,
        )

    @pl.loop(1, pieces)
    def _(o):
        d = exclusive_or(me, o, pieces)
        prepare(0, d, sends[0], d)

    pl.semaphore_wait(barrier, pieces + copies - 2)

    for d in partners(me, pieces):
        outward(0, d).start()

    for w in range(1, waves):
        @pl.loop(1, pieces)
        def _(o):
            d = exclusive_or(me, o, pieces)
            prepare(w, d, sends[w], d)

        for d in partners(me, pieces):
            outward(w, d).start()

    for w in range(waves):
        prepare(w, me, recvs[w], me)

    @pl.loop(0, pieces)
    def _(b):
        found = 0
        for d in range(pieces):
            found = jnp.where(block_ref[d] == b, d, found)
        places_ref[b] = found

    def build(g):
        taps = taps_ref[pl.ds(g, 1), :]
        kernel = (taps * scale_of(taps)).astype(BF16).astype(F32)
        return toeplitz_table(kernel, rows)

    early = min(EARLY, waves)

    @pl.loop(0, early * each // pair)
    def _(i):
        made = [build(i * pair + k) for k in range(pair)]
        for k in range(pair):
            tables_ref[i * pair + k] = made[k]

    def unload(w):
        @pl.loop(1, pieces)
        def _(o):
            arriving(w, lax.rem(me + pieces - o, pieces)).wait_recv()

        @pl.loop(0, pieces)
        def _(d):
            columns = pl.ds(pl.multiple_of(d * channels + w * part, 128), part)
            mixing_ref[:, columns] = homes[w][d, 0].T
            returned_ref[:, columns] = lax.dot_general(
                turn, homes[w][d, 1], (((1,), (1,)), ((), ())), preferred_element_type=F32
            ).astype(BF16)

    for w in range(waves):

        @pl.loop(1, pieces)
        def _(o):
            inward(w, lax.rem(me + pieces - o, pieces)).wait_recv()

        @pl.loop(0, pieces)
        def _(b):
            ordered_ref[b] = recvs[w][places_ref[b]]

        @pl.loop(0, each // pair)
        def _(i):
            made = []
            for k in range(pair):
                g = i * pair + k
                table = tables_ref[w * each + g] if w < early else build(w * each + g)
                lines = pl.ds(pl.multiple_of(g * size, size), size)
                signal = ordered_ref[:, 0, lines, :].reshape(pieces * size, rows)
                weighted = ordered_ref[:, 1, lines, :].reshape(pieces * size, rows)
                made.append((g, lines, *group_work(signal, weighted, table, pieces)))
            for g, lines, mixing, returned, sums in made:
                filtered_ref[:, 0, lines, :] = mixing.reshape(pieces, size, rows)
                filtered_ref[:, 1, lines, :] = returned.reshape(pieces, size, rows)
                lags[w][me_dp, pl.ds(g, 1), :] = sums

        @pl.loop(0, pieces)
        def _(d):
            results[w][d] = filtered_ref[block_ref[d]]

        for d in partners(me, pieces):
            homeward(w, d).start()

        @pl.loop(1, copies)
        def _(o):
            lag_copy(w, lax.rem(me_dp + o, copies), me_dp).start()

        homes[w][me] = results[w][me]
        if w > 0:
            unload(w - 1)

    def finish(w):
        @pl.loop(1, copies)
        def _(o):
            d = lax.rem(me_dp + copies - o, copies)
            lag_copy(w, d, d).wait_recv()

        total = lags[w][0]
        for i in range(1, copies):
            total = total + lags[w][i]
        turned = turning(rows, F32)
        mean = jnp.concatenate(
            [
                jnp.dot(
                    total[:, l * rows : (l + 1) * rows], turned,
                    precision=lax.Precision.HIGHEST, preferred_element_type=F32,
                )
                for l in reversed(range(pieces))
            ],
            axis=1,
        ) / copies
        taps = taps_ref[w * each : (w + 1) * each, :]
        scale = scale_of(taps)
        projection = jnp.sum(mean * taps, axis=1, keepdims=True)
        taps_grad_ref[w * each : (w + 1) * each, :] = (
            scale * mean - taps * (scale * scale * scale) * projection
        )

    for w in range(waves - 1):
        finish(w)
    unload(waves - 1)
    finish(waves - 1)

    for w in range(waves):

        @pl.loop(1, pieces)
        def _(o):
            d = lax.rem(me + o, pieces)
            outward(w, d).wait_send()
            homeward(w, d).wait_send()

        @pl.loop(1, copies)
        def _(o):
            lag_copy(w, lax.rem(me_dp + o, copies), me_dp).wait_send()


def shards(output_gate_input, key_input, value_input, upstream, filter_taps, block_of_shard):
    groups, length = filter_taps.shape
    pieces = block_of_shard.shape[0]
    copies = lax.axis_size("dp")
    gates, keys, values, grads = (
        member[0] for member in (output_gate_input, key_input, value_input, upstream)
    )
    rows, width = gates.shape
    channels = width // pieces
    part = 128
    waves = channels // part
    each = groups // waves
    vmem = pl.BlockSpec(memory_space=pltpu.VMEM)
    smem = pl.BlockSpec(memory_space=pltpu.SMEM)
    slots = pltpu.VMEM((pieces, 2, part, rows), BF16)
    ctx_sems = pltpu.SemaphoreType.DMA((waves, pieces))
    dp_sems = pltpu.SemaphoreType.DMA((waves, copies))
    mixing, returned, taps_grad = pl.pallas_call(
        functools.partial(layer, waves, pieces, copies),
        out_shape=(
            jax.ShapeDtypeStruct((rows, width), BF16),
            jax.ShapeDtypeStruct((rows, width), BF16),
            jax.ShapeDtypeStruct((groups, length), F32),
        ),
        in_specs=[smem] + [vmem] * 5,
        out_specs=(vmem,) * 3,
        scratch_shapes=[
            pltpu.SMEM((pieces,), jnp.int32),
            pltpu.VMEM((min(EARLY, waves) * each, rows, length), BF16),
            slots,
            slots,
            *([slots] * (4 * waves)),
            *([pltpu.VMEM((copies, each, length), F32)] * waves),
            ctx_sems, ctx_sems, ctx_sems, ctx_sems, dp_sems, dp_sems,
        ],
        compiler_params=pltpu.CompilerParams(
            vmem_limit_bytes=56 * 1024 * 1024, collective_id=0, has_side_effects=True
        ),
        cost_estimate=pl.CostEstimate(
            flops=6 * channels * length * length, bytes_accessed=12 * rows * width, transcendentals=0
        ),
    )(block_of_shard, filter_taps, gates, keys, values, grads)
    steps = 4
    wide = pl.BlockSpec((rows // steps, width), lambda i: (i, 0))
    whole = pl.BlockSpec((groups, length), lambda i: (0, 0))
    *outs, taps_grad = pl.pallas_call(
        products,
        grid=(steps,),
        out_shape=[jax.ShapeDtypeStruct((rows, width), BF16)] * 4
        + [jax.ShapeDtypeStruct((groups, length), F32)],
        in_specs=[wide] * 6 + [whole],
        out_specs=[wide] * 4 + [whole],
        compiler_params=pltpu.CompilerParams(vmem_limit_bytes=32 * 1024 * 1024),
    )(gates, grads, keys, values, mixing, returned, taps_grad)
    return (*(out[None] for out in outs), taps_grad)


def solution(mesh):
    wide = P("dp", "ctx", None)
    return jax.shard_map(
        shards,
        mesh=mesh,
        in_specs=(wide, wide, wide, wide, P("ctx", None), P()),
        out_specs=(wide, wide, wide, wide, P("ctx", None)),
        check_vma=False,
    )
```

```python
import functools
import math

import jax
import jax.numpy as jnp
from jax import lax
from jax.experimental import pallas as pl
from jax.experimental.pallas import tpu as pltpu
from jax.sharding import PartitionSpec as P

epsilon = 1e-06
F32 = jnp.float32
BF16 = jnp.bfloat16
EARLY = 2


def gate_product(first, second):
    return first * second


def toeplitz_table(row, rows):
    length = row.shape[1]
    spread = jnp.broadcast_to(row, (rows, length))
    rolled = pltpu.roll(spread, 0, 1, stride=1, stride_axis=0)
    lag = lax.broadcasted_iota(jnp.int32, (rows, rows), 1) - lax.broadcasted_iota(
        jnp.int32, (rows, rows), 0
    )
    first = jnp.where(lag >= 0, rolled[:, :rows], 0.0)
    return jnp.concatenate([first, rolled[:, rows:]], axis=1).astype(BF16)


def diagonal_sums(square):
    rows, length = square.shape
    total_index = lax.broadcasted_iota(jnp.int32, (rows, rows), 0) + lax.broadcasted_iota(
        jnp.int32, (rows, rows), 1
    )
    last = jnp.where(total_index < rows, square[:, length - rows :], 0.0)
    total = jnp.concatenate([square[:, : length - rows], last], axis=1)
    half = rows // 2
    while half >= 8:
        total = total[:half] + pltpu.roll(total[half:], half, 1)
        half //= 2
    while half >= 1:
        total = total + pltpu.roll(pltpu.roll(total, half, 1), 8 - half, 0)
        half //= 2
    return total[:1]


def turning(rows, kind):
    total_index = lax.broadcasted_iota(jnp.int32, (rows, rows), 0) + lax.broadcasted_iota(
        jnp.int32, (rows, rows), 1
    )
    return jnp.where(total_index == rows - 1, 1.0, 0.0).astype(kind)


def group_work(signal, weighted, table, pieces):
    lines, rows = signal.shape
    size = lines // pieces

    def later(l):
        return jnp.concatenate([jnp.zeros((l * size, rows), BF16), signal[: lines - l * size]], axis=0) if l else signal

    def earlier(l):
        return jnp.concatenate([weighted[l * size :], jnp.zeros((l * size, rows), BF16)], axis=0) if l else weighted

    ahead = [earlier(l) for l in range(pieces)]
    both = jnp.concatenate(
        [jnp.concatenate([later(l), ahead[l]], axis=0) for l in range(pieces)], axis=1
    )
    stacked = jnp.concatenate(
        [table[:, l * rows : (l + 1) * rows] for l in range(pieces)], axis=0
    )
    filtered = jnp.dot(both, stacked, preferred_element_type=F32).astype(BF16)
    square = lax.dot_general(
        signal,
        jnp.concatenate(ahead[::-1], axis=1),
        (((0,), (0,)), ((), ())),
        preferred_element_type=F32,
    )
    return filtered[:lines], filtered[lines:], diagonal_sums(square)


def scale_of(taps):
    mean = jnp.mean(taps * taps, axis=1, keepdims=True)
    return 1.0 / (math.sqrt(taps.shape[1]) * jnp.sqrt(mean + epsilon))


def exclusive_or(first, second, size):
    total, bit = 0, 1
    while bit < size:
        total = total + bit * lax.rem(first // bit + second // bit, 2)
        bit *= 2
    return total


def send_orders(pieces):
    half = pieces // 2
    chips = list(range(1, half))
    turned = [chips[1], chips[0], *chips[2:]] if len(chips) > 1 else chips
    one = [2 * c for c in chips] + [2 * c + 1 for c in chips] + [1]
    other = [2 * c + 1 for c in turned] + [2 * c for c in turned] + [1]
    return list(zip(one, other))


def partners(me, pieces):
    core = lax.rem(me, 2)
    for one, other in send_orders(pieces):
        yield exclusive_or(me, one + core * (other - one), pieces)


def products(gates, grads, keys, values, mixing, returned, taps, out, gate, key, value, taps_out):
    out[...] = gates[...] * mixing[...]
    gate[...] = grads[...] * mixing[...]
    key[...] = returned[...] * values[...]
    value[...] = returned[...] * keys[...]
    taps_out[...] = taps[...]


def layer(
    waves, pieces, copies,
    block_ref, taps_ref, gates_ref, keys_ref, values_ref, grads_ref,
    mixing_ref, returned_ref, taps_grad_ref,
    places_ref, tables_ref, ordered_ref, filtered_ref, *rest,
):
    sends, recvs, results, homes, lags = (rest[i * waves : (i + 1) * waves] for i in range(5))
    out_sem, in_sem, back_sem, home_sem, lag_out_sem, lag_in_sem = rest[5 * waves :]
    me = lax.axis_index("ctx")
    me_dp = lax.axis_index("dp")
    rows, width = gates_ref.shape
    channels = width // pieces
    part = channels // waves
    groups = taps_ref.shape[0]
    size = channels // groups
    each = groups // waves
    turn = turning(rows, BF16)
    pair = 2 if pieces <= 8 and each % 2 == 0 else 1

    barrier = pltpu.get_barrier_semaphore()

    @pl.loop(1, pieces)
    def _(o):
        pl.semaphore_signal(
            barrier, inc=1, device_id={"ctx": lax.rem(me + o, pieces)}, device_id_type=pl.DeviceIdType.MESH
        )

    @pl.loop(1, copies)
    def _(o):
        pl.semaphore_signal(
            barrier, inc=1, device_id={"dp": lax.rem(me_dp + o, copies)}, device_id_type=pl.DeviceIdType.MESH
        )

    def prepare(w, d, ref, slot):
        columns = pl.ds(pl.multiple_of(d * channels + w * part, 128), part)
        ref[slot, 0] = gate_product(keys_ref[:, columns], values_ref[:, columns]).T
        ref[slot, 1] = lax.dot_general(
            gate_product(grads_ref[:, columns], gates_ref[:, columns]), turn,
            (((0,), (0,)), ((), ())), preferred_element_type=F32,
        ).astype(BF16)

    def outward(w, d):
        return pltpu.make_async_remote_copy(
            src_ref=sends[w].at[d], dst_ref=recvs[w].at[me],
            send_sem=out_sem.at[w, d], recv_sem=in_sem.at[w, me],
            device_id={"ctx": d}, device_id_type=pl.DeviceIdType.MESH,
        )

    def inward(w, d):
        return pltpu.make_async_remote_copy(
            src_ref=sends[w].at[d], dst_ref=recvs[w].at[d],
            send_sem=out_sem.at[w, d], recv_sem=in_sem.at[w, d],
            device_id={"ctx": d}, device_id_type=pl.DeviceIdType.MESH,
        )

    def homeward(w, d):
        return pltpu.make_async_remote_copy(
            src_ref=results[w].at[d], dst_ref=homes[w].at[me],
            send_sem=back_sem.at[w, d], recv_sem=home_sem.at[w, me],
            device_id={"ctx": d}, device_id_type=pl.DeviceIdType.MESH,
        )

    def arriving(w, d):
        return pltpu.make_async_remote_copy(
            src_ref=results[w].at[d], dst_ref=homes[w].at[d],
            send_sem=back_sem.at[w, d], recv_sem=home_sem.at[w, d],
            device_id={"ctx": d}, device_id_type=pl.DeviceIdType.MESH,
        )

    def lag_copy(w, d, slot):
        return pltpu.make_async_remote_copy(
            src_ref=lags[w].at[me_dp], dst_ref=lags[w].at[slot],
            send_sem=lag_out_sem.at[w, d], recv_sem=lag_in_sem.at[w, slot],
            device_id={"dp": d}, device_id_type=pl.DeviceIdType.MESH,
        )

    @pl.loop(1, pieces)
    def _(o):
        d = exclusive_or(me, o, pieces)
        prepare(0, d, sends[0], d)

    pl.semaphore_wait(barrier, pieces + copies - 2)

    for d in partners(me, pieces):
        outward(0, d).start()

    for w in range(1, waves):
        @pl.loop(1, pieces)
        def _(o):
            d = exclusive_or(me, o, pieces)
            prepare(w, d, sends[w], d)

    for w in range(waves):
        prepare(w, me, recvs[w], me)

    @pl.loop(0, pieces)
    def _(b):
        found = 0
        for d in range(pieces):
            found = jnp.where(block_ref[d] == b, d, found)
        places_ref[b] = found

    def build(g):
        taps = taps_ref[pl.ds(g, 1), :]
        kernel = (taps * scale_of(taps)).astype(BF16).astype(F32)
        return toeplitz_table(kernel, rows)

    early = min(EARLY, waves)

    for w in range(early):

        @pl.loop(w * each // pair, (w + 1) * each // pair)
        def _(i):
            made = [build(i * pair + k) for k in range(pair)]
            for k in range(pair):
                tables_ref[i * pair + k] = made[k]

        if w == 0 and waves > 1:
            for d in partners(me, pieces):
                outward(1, d).start()

    def unload(w):
        @pl.loop(1, pieces)
        def _(o):
            arriving(w, lax.rem(me + pieces - o, pieces)).wait_recv()

        @pl.loop(0, pieces)
        def _(d):
            columns = pl.ds(pl.multiple_of(d * channels + w * part, 128), part)
            mixing_ref[:, columns] = homes[w][d, 0].T
            returned_ref[:, columns] = lax.dot_general(
                turn, homes[w][d, 1], (((1,), (1,)), ((), ())), preferred_element_type=F32
            ).astype(BF16)

    for w in range(waves):

        @pl.loop(1, pieces)
        def _(o):
            inward(w, lax.rem(me + pieces - o, pieces)).wait_recv()

        if w + 2 < waves:
            for d in partners(me, pieces):
                outward(w + 2, d).start()

        @pl.loop(0, pieces)
        def _(b):
            ordered_ref[b] = recvs[w][places_ref[b]]

        @pl.loop(0, each // pair)
        def _(i):
            made = []
            for k in range(pair):
                g = i * pair + k
                table = tables_ref[w * each + g] if w < early else build(w * each + g)
                lines = pl.ds(pl.multiple_of(g * size, size), size)
                signal = ordered_ref[:, 0, lines, :].reshape(pieces * size, rows)
                weighted = ordered_ref[:, 1, lines, :].reshape(pieces * size, rows)
                made.append((g, lines, *group_work(signal, weighted, table, pieces)))
            for g, lines, mixing, returned, sums in made:
                filtered_ref[:, 0, lines, :] = mixing.reshape(pieces, size, rows)
                filtered_ref[:, 1, lines, :] = returned.reshape(pieces, size, rows)
                lags[w][me_dp, pl.ds(g, 1), :] = sums

        @pl.loop(0, pieces)
        def _(d):
            results[w][d] = filtered_ref[block_ref[d]]

        for d in partners(me, pieces):
            homeward(w, d).start()

        @pl.loop(1, copies)
        def _(o):
            lag_copy(w, lax.rem(me_dp + o, copies), me_dp).start()

        homes[w][me] = results[w][me]
        if w > 0:
            unload(w - 1)

    def finish(w):
        @pl.loop(1, copies)
        def _(o):
            d = lax.rem(me_dp + copies - o, copies)
            lag_copy(w, d, d).wait_recv()

        total = lags[w][0]
        for i in range(1, copies):
            total = total + lags[w][i]
        turned = turning(rows, F32)
        mean = jnp.concatenate(
            [
                jnp.dot(
                    total[:, l * rows : (l + 1) * rows], turned,
                    precision=lax.Precision.HIGHEST, preferred_element_type=F32,
                )
                for l in reversed(range(pieces))
            ],
            axis=1,
        ) / copies
        taps = taps_ref[w * each : (w + 1) * each, :]
        scale = scale_of(taps)
        projection = jnp.sum(mean * taps, axis=1, keepdims=True)
        taps_grad_ref[w * each : (w + 1) * each, :] = (
            scale * mean - taps * (scale * scale * scale) * projection
        )

    for w in range(waves - 1):
        finish(w)
    unload(waves - 1)
    finish(waves - 1)

    for w in range(waves):

        @pl.loop(1, pieces)
        def _(o):
            d = lax.rem(me + o, pieces)
            outward(w, d).wait_send()
            homeward(w, d).wait_send()

        @pl.loop(1, copies)
        def _(o):
            lag_copy(w, lax.rem(me_dp + o, copies), me_dp).wait_send()


def shards(output_gate_input, key_input, value_input, upstream, filter_taps, block_of_shard):
    groups, length = filter_taps.shape
    pieces = block_of_shard.shape[0]
    copies = lax.axis_size("dp")
    gates, keys, values, grads = (
        member[0] for member in (output_gate_input, key_input, value_input, upstream)
    )
    rows, width = gates.shape
    channels = width // pieces
    part = 128
    waves = channels // part
    each = groups // waves
    vmem = pl.BlockSpec(memory_space=pltpu.VMEM)
    smem = pl.BlockSpec(memory_space=pltpu.SMEM)
    slots = pltpu.VMEM((pieces, 2, part, rows), BF16)
    ctx_sems = pltpu.SemaphoreType.DMA((waves, pieces))
    dp_sems = pltpu.SemaphoreType.DMA((waves, copies))
    mixing, returned, taps_grad = pl.pallas_call(
        functools.partial(layer, waves, pieces, copies),
        out_shape=(
            jax.ShapeDtypeStruct((rows, width), BF16),
            jax.ShapeDtypeStruct((rows, width), BF16),
            jax.ShapeDtypeStruct((groups, length), F32),
        ),
        in_specs=[smem] + [vmem] * 5,
        out_specs=(vmem,) * 3,
        scratch_shapes=[
            pltpu.SMEM((pieces,), jnp.int32),
            pltpu.VMEM((min(EARLY, waves) * each, rows, length), BF16),
            slots,
            slots,
            *([slots] * (4 * waves)),
            *([pltpu.VMEM((copies, each, length), F32)] * waves),
            ctx_sems, ctx_sems, ctx_sems, ctx_sems, dp_sems, dp_sems,
        ],
        compiler_params=pltpu.CompilerParams(
            vmem_limit_bytes=56 * 1024 * 1024, collective_id=0, has_side_effects=True
        ),
        cost_estimate=pl.CostEstimate(
            flops=6 * channels * length * length, bytes_accessed=12 * rows * width, transcendentals=0
        ),
    )(block_of_shard, filter_taps, gates, keys, values, grads)
    steps = 4
    wide = pl.BlockSpec((rows // steps, width), lambda i: (i, 0))
    whole = pl.BlockSpec((groups, length), lambda i: (0, 0))
    *outs, taps_grad = pl.pallas_call(
        products,
        grid=(steps,),
        out_shape=[jax.ShapeDtypeStruct((rows, width), BF16)] * 4
        + [jax.ShapeDtypeStruct((groups, length), F32)],
        in_specs=[wide] * 6 + [whole],
        out_specs=[wide] * 4 + [whole],
        compiler_params=pltpu.CompilerParams(vmem_limit_bytes=60 * 1024 * 1024),
    )(gates, grads, keys, values, mixing, returned, taps_grad)
    return (*(out[None] for out in outs), taps_grad)


def solution(mesh):
    wide = P("dp", "ctx", None)
    return jax.shard_map(
        shards,
        mesh=mesh,
        in_specs=(wide, wide, wide, wide, P("ctx", None), P()),
        out_specs=(wide, wide, wide, wide, P("ctx", None)),
        check_vma=False,
    )
```

```python
import functools
import math

import jax
import jax.numpy as jnp
from jax import lax
from jax.experimental import pallas as pl
from jax.experimental.pallas import tpu as pltpu
from jax.sharding import PartitionSpec as P

epsilon = 1e-06
F32 = jnp.float32
BF16 = jnp.bfloat16
EARLY = 2


def gate_product(first, second):
    return first * second


def toeplitz_table(row, rows):
    length = row.shape[1]
    spread = jnp.broadcast_to(row, (rows, length))
    rolled = pltpu.roll(spread, 0, 1, stride=1, stride_axis=0)
    lag = lax.broadcasted_iota(jnp.int32, (rows, rows), 1) - lax.broadcasted_iota(
        jnp.int32, (rows, rows), 0
    )
    first = jnp.where(lag >= 0, rolled[:, :rows], 0.0)
    return jnp.concatenate([first, rolled[:, rows:]], axis=1).astype(BF16)


def diagonal_sums(square):
    rows, length = square.shape
    total_index = lax.broadcasted_iota(jnp.int32, (rows, rows), 0) + lax.broadcasted_iota(
        jnp.int32, (rows, rows), 1
    )
    last = jnp.where(total_index < rows, square[:, length - rows :], 0.0)
    total = jnp.concatenate([square[:, : length - rows], last], axis=1)
    half = rows // 2
    while half >= 8:
        total = total[:half] + pltpu.roll(total[half:], half, 1)
        half //= 2
    while half >= 1:
        total = total + pltpu.roll(pltpu.roll(total, half, 1), 8 - half, 0)
        half //= 2
    return total[:1]


def turning(rows, kind):
    total_index = lax.broadcasted_iota(jnp.int32, (rows, rows), 0) + lax.broadcasted_iota(
        jnp.int32, (rows, rows), 1
    )
    return jnp.where(total_index == rows - 1, 1.0, 0.0).astype(kind)


def group_work(signal, weighted, table, pieces):
    lines, rows = signal.shape
    size = lines // pieces

    def later(l):
        return jnp.concatenate([jnp.zeros((l * size, rows), BF16), signal[: lines - l * size]], axis=0) if l else signal

    def earlier(l):
        return jnp.concatenate([weighted[l * size :], jnp.zeros((l * size, rows), BF16)], axis=0) if l else weighted

    ahead = [earlier(l) for l in range(pieces)]
    both = jnp.concatenate(
        [jnp.concatenate([later(l), ahead[l]], axis=0) for l in range(pieces)], axis=1
    )
    stacked = jnp.concatenate(
        [table[:, l * rows : (l + 1) * rows] for l in range(pieces)], axis=0
    )
    filtered = jnp.dot(both, stacked, preferred_element_type=F32).astype(BF16)
    square = lax.dot_general(
        signal,
        jnp.concatenate(ahead[::-1], axis=1),
        (((0,), (0,)), ((), ())),
        preferred_element_type=F32,
    )
    return filtered[:lines], filtered[lines:], diagonal_sums(square)


def scale_of(taps):
    mean = jnp.mean(taps * taps, axis=1, keepdims=True)
    return 1.0 / (math.sqrt(taps.shape[1]) * jnp.sqrt(mean + epsilon))


def exclusive_or(first, second, size):
    total, bit = 0, 1
    while bit < size:
        total = total + bit * lax.rem(first // bit + second // bit, 2)
        bit *= 2
    return total


def send_orders(pieces):
    half = pieces // 2
    chips = list(range(1, half))
    turned = [chips[1], chips[0], *chips[2:]] if len(chips) > 1 else chips
    one = [2 * c for c in chips] + [2 * c + 1 for c in chips] + [1]
    other = [2 * c + 1 for c in turned] + [2 * c for c in turned] + [1]
    return list(zip(one, other))


def partners(me, pieces):
    core = lax.rem(me, 2)
    for one, other in send_orders(pieces):
        yield exclusive_or(me, one + core * (other - one), pieces)


def products(gates, grads, keys, values, mixing, returned, taps, out, gate, key, value, taps_out):
    out[...] = gates[...] * mixing[...]
    gate[...] = grads[...] * mixing[...]
    key[...] = returned[...] * values[...]
    value[...] = returned[...] * keys[...]
    taps_out[...] = taps[...]


def layer(
    waves, pieces, copies,
    block_ref, taps_ref, gates_ref, keys_ref, values_ref, grads_ref,
    mixing_ref, returned_ref, taps_grad_ref,
    places_ref, tables_ref, ordered_ref, filtered_ref, *rest,
):
    sends, recvs, results, homes, lags = (rest[i * waves : (i + 1) * waves] for i in range(5))
    out_sem, in_sem, back_sem, home_sem, lag_out_sem, lag_in_sem = rest[5 * waves :]
    me = lax.axis_index("ctx")
    me_dp = lax.axis_index("dp")
    rows, width = gates_ref.shape
    channels = width // pieces
    part = channels // waves
    groups = taps_ref.shape[0]
    size = channels // groups
    each = groups // waves
    turn = turning(rows, BF16)
    pair = 4 if pieces <= 8 and each % 4 == 0 else 1

    barrier = pltpu.get_barrier_semaphore()

    @pl.loop(1, pieces)
    def _(o):
        pl.semaphore_signal(
            barrier, inc=1, device_id={"ctx": lax.rem(me + o, pieces)}, device_id_type=pl.DeviceIdType.MESH
        )

    @pl.loop(1, copies)
    def _(o):
        pl.semaphore_signal(
            barrier, inc=1, device_id={"dp": lax.rem(me_dp + o, copies)}, device_id_type=pl.DeviceIdType.MESH
        )

    def prepare(w, d, ref, slot):
        columns = pl.ds(pl.multiple_of(d * channels + w * part, 128), part)
        ref[slot, 0] = gate_product(keys_ref[:, columns], values_ref[:, columns]).T
        ref[slot, 1] = lax.dot_general(
            gate_product(grads_ref[:, columns], gates_ref[:, columns]), turn,
            (((0,), (0,)), ((), ())), preferred_element_type=F32,
        ).astype(BF16)

    def outward(w, d):
        return pltpu.make_async_remote_copy(
            src_ref=sends[w].at[d], dst_ref=recvs[w].at[me],
            send_sem=out_sem.at[w, d], recv_sem=in_sem.at[w, me],
            device_id={"ctx": d}, device_id_type=pl.DeviceIdType.MESH,
        )

    def inward(w, d):
        return pltpu.make_async_remote_copy(
            src_ref=sends[w].at[d], dst_ref=recvs[w].at[d],
            send_sem=out_sem.at[w, d], recv_sem=in_sem.at[w, d],
            device_id={"ctx": d}, device_id_type=pl.DeviceIdType.MESH,
        )

    def homeward(w, d):
        return pltpu.make_async_remote_copy(
            src_ref=results[w].at[d], dst_ref=homes[w].at[me],
            send_sem=back_sem.at[w, d], recv_sem=home_sem.at[w, me],
            device_id={"ctx": d}, device_id_type=pl.DeviceIdType.MESH,
        )

    def arriving(w, d):
        return pltpu.make_async_remote_copy(
            src_ref=results[w].at[d], dst_ref=homes[w].at[d],
            send_sem=back_sem.at[w, d], recv_sem=home_sem.at[w, d],
            device_id={"ctx": d}, device_id_type=pl.DeviceIdType.MESH,
        )

    def lag_copy(w, d, slot):
        return pltpu.make_async_remote_copy(
            src_ref=lags[w].at[me_dp], dst_ref=lags[w].at[slot],
            send_sem=lag_out_sem.at[w, d], recv_sem=lag_in_sem.at[w, slot],
            device_id={"dp": d}, device_id_type=pl.DeviceIdType.MESH,
        )

    @pl.loop(1, pieces)
    def _(o):
        d = exclusive_or(me, o, pieces)
        prepare(0, d, sends[0], d)

    pl.semaphore_wait(barrier, pieces + copies - 2)

    for d in partners(me, pieces):
        outward(0, d).start()

    for w in range(1, waves):
        @pl.loop(1, pieces)
        def _(o):
            d = exclusive_or(me, o, pieces)
            prepare(w, d, sends[w], d)

    for w in range(waves):
        prepare(w, me, recvs[w], me)

    @pl.loop(0, pieces)
    def _(b):
        found = 0
        for d in range(pieces):
            found = jnp.where(block_ref[d] == b, d, found)
        places_ref[b] = found

    def build(g):
        taps = taps_ref[pl.ds(g, 1), :]
        kernel = (taps * scale_of(taps)).astype(BF16).astype(F32)
        return toeplitz_table(kernel, rows)

    early = min(EARLY, waves)

    for w in range(early):

        @pl.loop(w * each // pair, (w + 1) * each // pair)
        def _(i):
            made = [build(i * pair + k) for k in range(pair)]
            for k in range(pair):
                tables_ref[i * pair + k] = made[k]

        if w == 0 and waves > 1:
            for d in partners(me, pieces):
                outward(1, d).start()

    def unload(w):
        @pl.loop(1, pieces)
        def _(o):
            arriving(w, lax.rem(me + pieces - o, pieces)).wait_recv()

        @pl.loop(0, pieces)
        def _(d):
            columns = pl.ds(pl.multiple_of(d * channels + w * part, 128), part)
            mixing_ref[:, columns] = homes[w][d, 0].T
            returned_ref[:, columns] = lax.dot_general(
                turn, homes[w][d, 1], (((1,), (1,)), ((), ())), preferred_element_type=F32
            ).astype(BF16)

    for w in range(waves):

        @pl.loop(1, pieces)
        def _(o):
            inward(w, lax.rem(me + pieces - o, pieces)).wait_recv()

        if w + 2 < waves:
            for d in partners(me, pieces):
                outward(w + 2, d).start()

        @pl.loop(0, pieces)
        def _(b):
            ordered_ref[b] = recvs[w][places_ref[b]]

        @pl.loop(0, each // pair)
        def _(i):
            made = []
            for k in range(pair):
                g = i * pair + k
                table = tables_ref[w * each + g] if w < early else build(w * each + g)
                lines = pl.ds(pl.multiple_of(g * size, size), size)
                signal = ordered_ref[:, 0, lines, :].reshape(pieces * size, rows)
                weighted = ordered_ref[:, 1, lines, :].reshape(pieces * size, rows)
                made.append((g, lines, *group_work(signal, weighted, table, pieces)))
            for g, lines, mixing, returned, sums in made:
                filtered_ref[:, 0, lines, :] = mixing.reshape(pieces, size, rows)
                filtered_ref[:, 1, lines, :] = returned.reshape(pieces, size, rows)
                lags[w][me_dp, pl.ds(g, 1), :] = sums

        @pl.loop(0, pieces)
        def _(d):
            results[w][d] = filtered_ref[block_ref[d]]

        for d in partners(me, pieces):
            homeward(w, d).start()

        @pl.loop(1, copies)
        def _(o):
            lag_copy(w, lax.rem(me_dp + o, copies), me_dp).start()

        homes[w][me] = results[w][me]
        if w > 0:
            unload(w - 1)

    def finish(w):
        @pl.loop(1, copies)
        def _(o):
            d = lax.rem(me_dp + copies - o, copies)
            lag_copy(w, d, d).wait_recv()

        total = lags[w][0]
        for i in range(1, copies):
            total = total + lags[w][i]
        turned = turning(rows, F32)
        mean = jnp.concatenate(
            [
                jnp.dot(
                    total[:, l * rows : (l + 1) * rows], turned,
                    precision=lax.Precision.HIGHEST, preferred_element_type=F32,
                )
                for l in reversed(range(pieces))
            ],
            axis=1,
        ) / copies
        taps = taps_ref[w * each : (w + 1) * each, :]
        scale = scale_of(taps)
        projection = jnp.sum(mean * taps, axis=1, keepdims=True)
        taps_grad_ref[w * each : (w + 1) * each, :] = (
            scale * mean - taps * (scale * scale * scale) * projection
        )

    for w in range(waves - 1):
        finish(w)
    unload(waves - 1)
    finish(waves - 1)

    for w in range(waves):

        @pl.loop(1, pieces)
        def _(o):
            d = lax.rem(me + o, pieces)
            outward(w, d).wait_send()
            homeward(w, d).wait_send()

        @pl.loop(1, copies)
        def _(o):
            lag_copy(w, lax.rem(me_dp + o, copies), me_dp).wait_send()


def shards(output_gate_input, key_input, value_input, upstream, filter_taps, block_of_shard):
    groups, length = filter_taps.shape
    pieces = block_of_shard.shape[0]
    copies = lax.axis_size("dp")
    gates, keys, values, grads = (
        member[0] for member in (output_gate_input, key_input, value_input, upstream)
    )
    rows, width = gates.shape
    channels = width // pieces
    part = 128
    waves = channels // part
    each = groups // waves
    vmem = pl.BlockSpec(memory_space=pltpu.VMEM)
    smem = pl.BlockSpec(memory_space=pltpu.SMEM)
    slots = pltpu.VMEM((pieces, 2, part, rows), BF16)
    ctx_sems = pltpu.SemaphoreType.DMA((waves, pieces))
    dp_sems = pltpu.SemaphoreType.DMA((waves, copies))
    mixing, returned, taps_grad = pl.pallas_call(
        functools.partial(layer, waves, pieces, copies),
        out_shape=(
            jax.ShapeDtypeStruct((rows, width), BF16),
            jax.ShapeDtypeStruct((rows, width), BF16),
            jax.ShapeDtypeStruct((groups, length), F32),
        ),
        in_specs=[smem] + [vmem] * 5,
        out_specs=(vmem,) * 3,
        scratch_shapes=[
            pltpu.SMEM((pieces,), jnp.int32),
            pltpu.VMEM((min(EARLY, waves) * each, rows, length), BF16),
            slots,
            slots,
            *([slots] * (4 * waves)),
            *([pltpu.VMEM((copies, each, length), F32)] * waves),
            ctx_sems, ctx_sems, ctx_sems, ctx_sems, dp_sems, dp_sems,
        ],
        compiler_params=pltpu.CompilerParams(
            vmem_limit_bytes=56 * 1024 * 1024, collective_id=0, has_side_effects=True
        ),
        cost_estimate=pl.CostEstimate(
            flops=6 * channels * length * length, bytes_accessed=12 * rows * width, transcendentals=0
        ),
    )(block_of_shard, filter_taps, gates, keys, values, grads)
    steps = 8
    wide = pl.BlockSpec((rows // steps, width), lambda i: (i, 0))
    whole = pl.BlockSpec((groups, length), lambda i: (0, 0))
    *outs, taps_grad = pl.pallas_call(
        products,
        grid=(steps,),
        out_shape=[jax.ShapeDtypeStruct((rows, width), BF16)] * 4
        + [jax.ShapeDtypeStruct((groups, length), F32)],
        in_specs=[wide] * 6 + [whole],
        out_specs=[wide] * 4 + [whole],
        compiler_params=pltpu.CompilerParams(vmem_limit_bytes=60 * 1024 * 1024),
    )(gates, grads, keys, values, mixing, returned, taps_grad)
    return (*(out[None] for out in outs), taps_grad)


def solution(mesh):
    wide = P("dp", "ctx", None)
    return jax.shard_map(
        shards,
        mesh=mesh,
        in_specs=(wide, wide, wide, wide, P("ctx", None), P()),
        out_specs=(wide, wide, wide, wide, P("ctx", None)),
        check_vma=False,
    )
```
